32 devices in a mesh: groups: 2 (over x), blk: 16 (over z, y, core).
Axes of the slice: x: 2, y: 2, z: 4, core: 2. Of those that a mesh axis runs over, the one named last changes fastest.
Arguments:
- grads: bfloat16 [192, 32768], P('groups', 'blk'), parts along dimension 0, may hold values from -6 to 6
- block_values: bfloat16 [4096, 128, 128], P('blk'), may hold values from -0.046875 to 0.046875
- block_rows: int32 [4096], P('blk'), may hold values from 0 to 15, as said below
- block_cols: int32 [4096], P('blk'), may hold values from 0 to 31
- block_counts: int32 [16], P('blk'), may hold values from 129 to 256, as said below
- inv_gram: bfloat16 [4096, 4096], P('blk'), may hold values from -0.09375 to 0.09375
- queries: bfloat16 [256, 4096], P(('groups', 'blk')), parts along dimension 0, may hold values from -0.09375 to 0.09375
Outputs:
- scores: float32 [192, 128], P(('groups', 'blk')), parts along dimension 0
The draws below stay inside these ranges and needn't reach their ends.
There are 2 independent parts, one for each index of `groups`. The reference program is written for one: setup_inputs(seed, part) draws one part's arguments, and reference() takes and returns one part's arrays. A program takes and returns all parts, laid end to end along the dimension named above; an argument that names none is the same for every part. Nothing has to cross between parts.
Inputs may be any that keep to these rules, and one draw needn't show every extreme that they name: `block_rows`: the slots of one parameter block name distinct pairs of block row and block column. The first block_counts[d] slots of parameter block d are used; some parameter block uses all 256.
All inputs are finite; a program needn't handle non-finite values.
Results may differ from the reference program's by a relative error of at most 0.0029.
Values may be sent and summed in bfloat16 or wider, within the bound.
A program may use at most 128 MiB of HBM per device.

```python
import jax
import jax.numpy as jnp
from jax import lax

P_DEV = 2048
NNZ_MAX = 256
K = 4096
B = 128
E = 96
NQ = 128
P_SIZE = 32768
SLOTS = 4096
N_BLK = 16


def pattern_positions(key):
    device_keys = jax.random.split(key, N_BLK)

    def one_device(device_key):
        return jax.random.permutation(device_key, P_DEV // B * (K // B))[:NNZ_MAX]
    return jax.vmap(one_device)(device_keys).reshape(-1).astype(jnp.int32)


def draw_block_rows(key, part):
    positions = pattern_positions(key)
    return (positions // (K // B)).astype(jnp.int32)


def draw_block_cols(key, part):
    positions = pattern_positions(key)
    return (positions % (K // B)).astype(jnp.int32)


def draw_block_counts(key, part):
    key = jax.random.fold_in(key, 7)
    short_key, full_key = jax.random.split(key)
    shortfall = jax.random.randint(short_key, (N_BLK,), 0, NNZ_MAX // 2)
    full_device = jax.random.randint(full_key, (), 0, N_BLK)
    device_ids = jnp.arange(N_BLK, dtype=jnp.int32)
    counts = jnp.where(device_ids == full_device, NNZ_MAX, NNZ_MAX - shortfall)
    return counts.astype(jnp.int32)


def block_levels(stream_key, shape, shards, least, top_value):
    level, own = 1.0, jax.random.fold_in(stream_key, 6)
    for position, shards_of in shards:
        steps = jnp.exp(jax.random.uniform(jax.random.fold_in(own, position), (shards_of,), jnp.float32, least / len(shards), top_value / len(shards)))
        level = level * jnp.repeat(steps, shape[position] // shards_of).reshape([-1 if axis == position else 1 for axis in range(len(shape))])
    return level


def centred(rng, extent, scale, most, shards=(), held_as=jnp.bfloat16):
    result = jax.random.normal(rng, extent, jnp.float32) * scale
    if len(shards) > 0:
        result = block_levels(rng, extent, shards, -0.22, 0.18) * result
    return jnp.clip(result, min=-most, max=most).astype(held_as)


def setup_inputs(seed: int = 0, part: int = 0) -> dict:
    arg_keys = jax.random.split(jax.random.key(seed), 8)
    part_keys = jax.random.split(jax.random.fold_in(arg_keys[7], part), 8)
    return {
        "grads": centred(part_keys[0], (E, P_SIZE), 1.0, 6.0, ((1, 16),)),
        "block_values": centred(arg_keys[1], (SLOTS, B, B), (SLOTS * B // (K // B)) ** -0.5, 0.046875, ((0, 16),)),
        "block_rows": draw_block_rows(jax.random.fold_in(arg_keys[7], 71), part),
        "block_cols": draw_block_cols(jax.random.fold_in(arg_keys[7], 71), part),
        "block_counts": draw_block_counts(jax.random.fold_in(arg_keys[7], 71), part),
        "inv_gram": centred(arg_keys[5], (K, K), K ** -0.5, 0.09375, ((0, 16),)),
        "queries": centred(part_keys[6], (NQ, K), K ** -0.5, 0.09375, ((0, 16),)),
    }


def reference(grads, block_values, block_rows, block_cols, block_counts, inv_gram, queries):
    col_blocks = K // B
    row_blocks = P_DEV // B
    param_shards = grads.astype(jnp.float32).reshape(E, N_BLK, row_blocks, B).transpose(1, 0, 2, 3)
    slot_values = block_values.reshape(N_BLK, NNZ_MAX, B, B)
    slot_rows = block_rows.reshape(N_BLK, NNZ_MAX).astype(jnp.int32)
    slot_cols = block_cols.reshape(N_BLK, NNZ_MAX).astype(jnp.int32)
    live_slots = (jnp.arange(NNZ_MAX, dtype=jnp.int32)[None, :] < block_counts[:, None]).astype(jnp.float32)

    def add_device(totals, inputs):
        param_shard, values_here, rows_here, cols_here, alive = inputs
        selected = jnp.take(param_shard, rows_here, axis=1)
        weights = values_here.astype(jnp.float32) * alive[:, None, None]
        products = jnp.einsum('ejb,jbc->ejc', selected, weights, precision=lax.Precision.HIGHEST)
        return totals.at[:, cols_here, :].add(products), None

    start_totals = jnp.zeros((E, col_blocks, B), jnp.float32)
    totals, unused = lax.scan(add_device, start_totals, (param_shards, slot_values, slot_rows, slot_cols, live_slots))
    features = totals.reshape(E, K)
    whitened_queries = lax.dot_general(inv_gram, queries, (((1,), (1,)), ((), ())), preferred_element_type=jnp.float32).astype(jnp.bfloat16)
    return jnp.dot(features, whitened_queries.astype(jnp.float32), precision=lax.Precision.HIGHEST)
```

```python
import functools

import jax
import jax.numpy as jnp
from jax import lax
from jax.experimental import pallas as pl
from jax.experimental.pallas import tpu as pltpu
from jax.sharding import PartitionSpec as P

MESH = pl.DeviceIdType.MESH
V_PIECES = 8


def passed_along(value, axis, by):
    devices = lax.axis_size(axis)
    return lax.ppermute(value, axis, [(i, (i + by) % devices) for i in range(devices)])


def cycle_tiles(moving, make_tile):
    cycle_size = lax.axis_size("blk")
    position = lax.axis_index("blk")
    first_tile = make_tile(moving)
    tile_stack = jnp.zeros((cycle_size,) + first_tile.shape, jnp.float32)
    tile_stack = lax.dynamic_update_index_in_dim(tile_stack, first_tile, position, 0)

    def advance_one(step_index, carry):
        stack_now, current = carry
        current = passed_along(current, "blk", 1)
        stack_now = lax.dynamic_update_index_in_dim(
            stack_now, make_tile(current), (position - step_index) % cycle_size, 0
        )
        return (stack_now, current)

    tile_stack = lax.fori_loop(1, cycle_size, advance_one, (tile_stack, moving))[0]
    return tile_stack


def shards(grads, block_values, block_rows, block_cols, block_counts, inv_gram, queries):
    examples, param_width = grads.shape
    slot_count = block_values.shape[0]
    block_side = block_values.shape[1]
    feature_dim = inv_gram.shape[1]
    col_blocks = feature_dim // block_side
    tiled = grads.reshape(examples, param_width // block_side, block_side)
    slot_group = 64
    group_count = slot_count // slot_group
    live_slots = (jnp.arange(slot_count, dtype=jnp.int32) < block_counts[0]).astype(jnp.bfloat16)

    def add_group(totals, inputs):
        group_rows, group_cols, group_values, group_live = inputs
        selected = jnp.take(tiled, group_rows, axis=1)
        weights = group_values * group_live[:, None, None]
        products = jnp.einsum("ejb,jbc->ejc", selected, weights, preferred_element_type=jnp.float32)
        return (totals.at[:, group_cols, :].add(products), None)

    group_inputs = (
        block_rows.reshape(group_count, slot_group),
        block_cols.reshape(group_count, slot_group),
        block_values.reshape(group_count, slot_group, block_side, block_side),
        live_slots.reshape(group_count, slot_group),
    )
    start_totals = jnp.zeros((examples, col_blocks, block_side), jnp.float32)
    totals, unused = lax.scan(add_group, start_totals, group_inputs)
    partial_features = totals.reshape(examples, feature_dim)
    contract = (((1,), (1,)), ((), ()))

    def tile_for_queries(query_block):
        return lax.dot_general(inv_gram, query_block, contract, preferred_element_type=jnp.float32)

    tile_stack = cycle_tiles(queries, tile_for_queries)
    gram_rows = inv_gram.shape[0]
    whitened_queries = (
        jnp.transpose(tile_stack, (1, 0, 2)).reshape(gram_rows, -1).astype(jnp.bfloat16)
    )
    features = lax.psum_scatter(partial_features, "blk", scatter_dimension=1, tiled=True)
    query_float = whitened_queries.astype(jnp.float32)
    return lax.psum_scatter(
        jnp.dot(features, query_float, precision=lax.Precision.HIGHEST),
        "blk",
        scatter_dimension=0,
        tiled=True,
    )


def remote(src, dst, send_sem, recv_sem, device):
    return pltpu.make_async_remote_copy(
        src_ref=src,
        dst_ref=dst,
        send_sem=send_sem,
        recv_sem=recv_sem,
        device_id={"blk": device},
        device_id_type=MESH,
    )


def fused_kernel(
    n, table, grads, values_hbm, gram_hbm, queries, out,
    values, gram, all_queries, pair_out, pair_in, far_out, far_in, score_out, score_in,
    values_sem, gram_sem, query_send, query_recv, pass_send, pair_send, pair_recv,
    far_send, far_recv, score_send, score_recv,
):
    chips = n // 2
    me = lax.axis_index("blk")
    chip = me // 2
    core = me % 2
    sibling = 2 * chip + 1 - core
    examples, params = grads.shape
    slots, side = values_hbm.shape[0], values_hbm.shape[1]
    width, feature_dim = gram.shape
    wide = width // side
    col_blocks = feature_dim // side
    row_blocks = params // side
    half = feature_dim // 2
    query_rows = queries.shape[0]
    out_rows = out.shape[0]
    piece = slots // V_PIECES

    barrier = pltpu.get_barrier_semaphore()

    def greet(k, _):
        pl.semaphore_signal(barrier, inc=1, device_id={"blk": (me + k) % n}, device_id_type=MESH)
        return 0

    lax.fori_loop(1, n, greet, 0)

    def values_copy(i):
        part = pl.ds(i * piece, piece)
        return pltpu.make_async_copy(values_hbm.at[part], values.at[part], values_sem.at[i])

    for i in range(V_PIECES):
        values_copy(i).start()
    gram_copy = pltpu.make_async_copy(gram_hbm, gram, gram_sem)
    gram_copy.start()

    own_queries = queries[...].astype(jnp.float32)
    all_queries[me] = jnp.concatenate(
        [own_queries[:, :half], own_queries[:, half:]], axis=0
    ).astype(jnp.bfloat16)
    values[slots] = jnp.zeros((side, side), jnp.bfloat16)
    pl.semaphore_wait(barrier, n - 1)

    def query_copy(k, to, which, sems):
        return remote(all_queries.at[which], all_queries.at[which], sems.at[k], query_recv.at[which], to)

    query_copy(0, sibling, me, query_send).start()

    def send_queries(k, _):
        query_copy(k, 2 * ((chip + k) % chips) + core, me, query_send).start()
        return 0

    lax.fori_loop(1, chips, send_queries, 0)

    for i in range(V_PIECES):
        values_copy(i).wait()

    def partial(owner):
        total = jnp.zeros((examples, width), jnp.float32)
        for r in range(0, row_blocks, 2):
            tile = jnp.concatenate(
                [
                    jnp.concatenate(
                        [values[table[(r + i) * col_blocks + owner * wide + j]] for j in range(wide)], axis=1
                    )
                    for i in range(2)
                ],
                axis=0,
            )
            total += jnp.dot(
                grads[:, r * side : (r + 2) * side], tile, preferred_element_type=jnp.float32
            )
        return total

    def pair_copy(k):
        return remote(pair_out.at[k], pair_in.at[k], pair_send.at[k], pair_recv.at[k], sibling)

    def for_sibling(k, _):
        owner = 2 * ((chip + 1 + k) % chips) + 1 - core
        pair_out[k] = partial(owner)
        pair_copy(k).start()
        return 0

    lax.fori_loop(0, chips, for_sibling, 0)

    def far_copy(k):
        to = 2 * ((chip + 1 + k) % chips) + core
        return remote(far_out.at[k], far_in.at[k], far_send.at[k], far_recv.at[k], to)

    def for_far(k, _):
        total = partial(2 * ((chip + 1 + k) % chips) + core)
        pair_copy(k).wait_recv()
        far_out[k] = (total + pair_in[k]).astype(jnp.bfloat16)
        far_copy(k).start()
        return 0

    lax.fori_loop(0, chips - 1, for_far, 0)
    features = partial(me)
    pair_copy(chips - 1).wait_recv()
    features += pair_in[chips - 1]

    def pass_queries(k, _):
        which = 2 * ((chip + chips - k) % chips) + core
        query_copy(k, sibling, which, pass_send).wait_recv()
        query_copy(k, sibling, which, pass_send).start()
        return 0

    lax.fori_loop(1, chips, pass_queries, 0)

    def wait_passed(k, _):
        which = 2 * ((chip + chips - k) % chips) + 1 - core
        query_copy(k, sibling, which, pass_send).wait_recv()
        return 0

    lax.fori_loop(0, chips, wait_passed, 0)
    gram_copy.wait()

    stacked = all_queries[...].reshape(n * 2 * query_rows, half)
    contract = (((1,), (1,)), ((), ()))
    first = lax.dot_general(gram[:, :half], stacked, contract, preferred_element_type=jnp.float32)
    second = lax.dot_general(gram[:, half:], stacked, contract, preferred_element_type=jnp.float32)
    columns = n * 2 * query_rows
    whitened = (first + pltpu.roll(second, columns - query_rows, 1)).astype(jnp.bfloat16)
    row = lax.broadcasted_iota(jnp.int32, (columns, n * query_rows), 0)
    col = lax.broadcasted_iota(jnp.int32, (columns, n * query_rows), 1)
    pick = (row == (col // query_rows) * (2 * query_rows) + col % query_rows).astype(jnp.bfloat16)
    whitened = jnp.dot(whitened, pick, preferred_element_type=jnp.float32).astype(jnp.bfloat16)

    for k in range(chips - 1):
        far_copy(k).wait_recv()
        features += far_in[k].astype(jnp.float32)
    high = features.astype(jnp.bfloat16)
    rest = features - high.astype(jnp.float32)
    middle = rest.astype(jnp.bfloat16)
    low = (rest - middle.astype(jnp.float32)).astype(jnp.bfloat16)
    scores = jnp.dot(high, whitened, preferred_element_type=jnp.float32)
    scores += jnp.dot(middle, whitened, preferred_element_type=jnp.float32)
    scores += jnp.dot(low, whitened, preferred_element_type=jnp.float32)
    for d in range(n):
        score_out[d, :out_rows, :] = scores[d * out_rows : (d + 1) * out_rows]

    def score_copy(k):
        to = (me + k) % n
        return remote(score_out.at[to], score_in.at[k], score_send.at[k], score_recv.at[k], to)

    def send_scores(k, _):
        score_copy(k).start()
        return 0

    lax.fori_loop(1, n, send_scores, 0)
    result = score_out[me]
    for k in range(1, n):
        score_copy(k).wait_recv()
        result += score_in[k]
    out[...] = result[:out_rows]

    def drain(k, _):
        query_copy(k, sibling, me, query_send).wait_send()
        pair_copy(k).wait_send()
        return 0

    lax.fori_loop(0, chips, drain, 0)

    def drain_far(k, _):
        far_copy(k).wait_send()
        query_copy(k + 1, sibling, me, pass_send).wait_send()
        return 0

    lax.fori_loop(0, chips - 1, drain_far, 0)

    def drain_scores(k, _):
        score_copy(k).wait_send()
        return 0

    lax.fori_loop(1, n, drain_scores, 0)


def fused_shards(grads, block_values, block_rows, block_cols, block_counts, inv_gram, queries):
    n = lax.axis_size("blk")
    chips = n // 2
    examples, params = grads.shape
    slots, side = block_values.shape[0], block_values.shape[1]
    width, feature_dim = inv_gram.shape
    query_rows = queries.shape[0]
    out_rows = examples // n
    padded_rows = -(-out_rows // 8) * 8
    places = (params // side) * (feature_dim // side)
    slot_ids = jnp.arange(slots, dtype=jnp.int32)
    place = jnp.where(slot_ids < block_counts[0], block_rows * (feature_dim // side) + block_cols, -1)
    hit = place[None, :] == jnp.arange(places, dtype=jnp.int32)[:, None]
    table = jnp.sum(jnp.where(hit, slot_ids[None, :] - slots, 0), axis=1) + slots
    vmem = pl.BlockSpec(memory_space=pltpu.VMEM)
    anywhere = pl.BlockSpec(memory_space=pl.ANY)
    dma = pltpu.SemaphoreType.DMA
    return pl.pallas_call(
        functools.partial(fused_kernel, n),
        out_shape=jax.ShapeDtypeStruct((out_rows, n * query_rows), jnp.float32),
        in_specs=[pl.BlockSpec(memory_space=pltpu.SMEM), vmem, anywhere, anywhere, vmem],
        out_specs=vmem,
        scratch_shapes=[
            pltpu.VMEM((slots + 1, side, side), jnp.bfloat16),
            pltpu.VMEM((width, feature_dim), jnp.bfloat16),
            pltpu.VMEM((n, 2 * query_rows, feature_dim // 2), jnp.bfloat16),
            pltpu.VMEM((chips, examples, width), jnp.float32),
            pltpu.VMEM((chips, examples, width), jnp.float32),
            pltpu.VMEM((chips, examples, width), jnp.bfloat16),
            pltpu.VMEM((chips, examples, width), jnp.bfloat16),
            pltpu.VMEM((n, padded_rows, n * query_rows), jnp.float32),
            pltpu.VMEM((n, padded_rows, n * query_rows), jnp.float32),
            dma((V_PIECES,)),
            dma(()),
            dma((chips,)),
            dma((n,)),
            dma((chips,)),
            dma((chips,)),
            dma((chips,)),
            dma((chips,)),
            dma((chips,)),
            dma((n,)),
            dma((n,)),
        ],
        compiler_params=pltpu.CompilerParams(
            collective_id=0, has_side_effects=True, vmem_limit_bytes=48 * 1024 * 1024
        ),
    )(table, grads, block_values, inv_gram, queries)


def fits(mesh, args):
    grads, block_values, _, _, _, inv_gram, queries = args
    n, groups = mesh.shape["blk"], mesh.shape["groups"]
    side = block_values.shape[1]
    width = inv_gram.shape[0] // n
    return (
        n % 2 == 0
        and width % side == 0
        and grads.shape[0] // groups % 16 == 0
        and queries.shape[0] // (groups * n) == 8
    )


def solution(mesh):
    placed = (
        P("groups", "blk"),
        P("blk", None, None),
        P("blk"),
        P("blk"),
        P("blk"),
        P("blk", None),
        P(("groups", "blk"), None),
    )

    def whole(*args):
        body = fused_shards if fits(mesh, args) else shards
        return jax.shard_map(
            body, mesh=mesh, in_specs=placed, out_specs=P(("groups", "blk"), None), check_vma=False
        )(*args)

    return whole
```

```python
import functools

import jax
import jax.numpy as jnp
from jax import lax
from jax.experimental import pallas as pl
from jax.experimental.pallas import tpu as pltpu
from jax.sharding import PartitionSpec as P

MESH = pl.DeviceIdType.MESH
V_PIECES = 8


def passed_along(value, axis, by):
    devices = lax.axis_size(axis)
    return lax.ppermute(value, axis, [(i, (i + by) % devices) for i in range(devices)])


def cycle_tiles(moving, make_tile):
    cycle_size = lax.axis_size("blk")
    position = lax.axis_index("blk")
    first_tile = make_tile(moving)
    tile_stack = jnp.zeros((cycle_size,) + first_tile.shape, jnp.float32)
    tile_stack = lax.dynamic_update_index_in_dim(tile_stack, first_tile, position, 0)

    def advance_one(step_index, carry):
        stack_now, current = carry
        current = passed_along(current, "blk", 1)
        stack_now = lax.dynamic_update_index_in_dim(
            stack_now, make_tile(current), (position - step_index) % cycle_size, 0
        )
        return (stack_now, current)

    tile_stack = lax.fori_loop(1, cycle_size, advance_one, (tile_stack, moving))[0]
    return tile_stack


def shards(grads, block_values, block_rows, block_cols, block_counts, inv_gram, queries):
    examples, param_width = grads.shape
    slot_count = block_values.shape[0]
    block_side = block_values.shape[1]
    feature_dim = inv_gram.shape[1]
    col_blocks = feature_dim // block_side
    tiled = grads.reshape(examples, param_width // block_side, block_side)
    slot_group = 64
    group_count = slot_count // slot_group
    live_slots = (jnp.arange(slot_count, dtype=jnp.int32) < block_counts[0]).astype(jnp.bfloat16)

    def add_group(totals, inputs):
        group_rows, group_cols, group_values, group_live = inputs
        selected = jnp.take(tiled, group_rows, axis=1)
        weights = group_values * group_live[:, None, None]
        products = jnp.einsum("ejb,jbc->ejc", selected, weights, preferred_element_type=jnp.float32)
        return (totals.at[:, group_cols, :].add(products), None)

    group_inputs = (
        block_rows.reshape(group_count, slot_group),
        block_cols.reshape(group_count, slot_group),
        block_values.reshape(group_count, slot_group, block_side, block_side),
        live_slots.reshape(group_count, slot_group),
    )
    start_totals = jnp.zeros((examples, col_blocks, block_side), jnp.float32)
    totals, unused = lax.scan(add_group, start_totals, group_inputs)
    partial_features = totals.reshape(examples, feature_dim)
    contract = (((1,), (1,)), ((), ()))

    def tile_for_queries(query_block):
        return lax.dot_general(inv_gram, query_block, contract, preferred_element_type=jnp.float32)

    tile_stack = cycle_tiles(queries, tile_for_queries)
    gram_rows = inv_gram.shape[0]
    whitened_queries = (
        jnp.transpose(tile_stack, (1, 0, 2)).reshape(gram_rows, -1).astype(jnp.bfloat16)
    )
    features = lax.psum_scatter(partial_features, "blk", scatter_dimension=1, tiled=True)
    query_float = whitened_queries.astype(jnp.float32)
    return lax.psum_scatter(
        jnp.dot(features, query_float, precision=lax.Precision.HIGHEST),
        "blk",
        scatter_dimension=0,
        tiled=True,
    )


def remote(src, dst, send_sem, recv_sem, device):
    return pltpu.make_async_remote_copy(
        src_ref=src,
        dst_ref=dst,
        send_sem=send_sem,
        recv_sem=recv_sem,
        device_id={"blk": device},
        device_id_type=MESH,
    )


def fused_kernel(
    n, rows_hbm, cols_hbm, counts, grads_hbm, values_hbm, gram_hbm, queries, out,
    rows, cols, table_rows, table, grads, values, gram, all_queries, pair_out, pair_in,
    near_out, near_in, far_out, far_in, score_out, score_in,
    slot_sems, values_sem, load_sems, query_send, query_recv, pass_near, pass_far, pass_pair,
    pair_send, pair_recv, near_send, near_recv, far_send, far_recv, score_send, score_recv,
):
    depth = n // 4
    me = lax.axis_index("blk")
    z, y, core = me // 4, (me // 2) % 2, me % 2

    def device(at_z, at_y, at_core):
        return 4 * at_z + 2 * at_y + at_core

    sibling = device(z, y, 1 - core)
    across = device(z, 1 - y, core)
    examples, params = grads.shape
    slots, side = values_hbm.shape[0], values_hbm.shape[1]
    width, feature_dim = gram.shape
    wide = width // side
    col_blocks = feature_dim // side
    row_blocks = params // side
    half = feature_dim // 2
    query_rows = queries.shape[0]
    out_rows = out.shape[0]
    piece = slots // V_PIECES
    lanes = rows.shape[1]

    barrier = pltpu.get_barrier_semaphore()

    def greet(k, _):
        pl.semaphore_signal(barrier, inc=1, device_id={"blk": (me + k) % n}, device_id_type=MESH)
        return 0

    lax.fori_loop(1, n, greet, 0)

    rows_copy = pltpu.make_async_copy(rows_hbm, rows, slot_sems.at[0])
    cols_copy = pltpu.make_async_copy(cols_hbm, cols, slot_sems.at[1])
    rows_copy.start()
    cols_copy.start()

    def values_copy(i):
        part = pl.ds(i * piece, piece)
        return pltpu.make_async_copy(values_hbm.at[part], values.at[part], values_sem.at[i])

    grads_copy = pltpu.make_async_copy(grads_hbm, grads, load_sems.at[0])
    gram_copy = pltpu.make_async_copy(gram_hbm, gram, load_sems.at[1])
    grads_copy.start()
    for i in range(V_PIECES):
        values_copy(i).start()
    gram_copy.start()

    own_queries = queries[...].astype(jnp.float32)
    all_queries[me] = jnp.concatenate(
        [own_queries[:, :half], own_queries[:, half:]], axis=0
    ).astype(jnp.bfloat16)
    values[slots] = jnp.zeros((side, side), jnp.bfloat16)
    pl.semaphore_wait(barrier, n - 1)

    def query_copy(which, to, send_sem):
        return remote(all_queries.at[which], all_queries.at[which], send_sem, query_recv.at[which], to)

    def send_queries(k, _):
        query_copy(me, device((z + k) % depth, y, core), query_send.at[k]).start()
        return 0

    lax.fori_loop(1, depth, send_queries, 0)
    query_copy(me, across, query_send.at[depth]).start()
    query_copy(me, sibling, query_send.at[0]).start()

    rows_copy.wait()
    cols_copy.wait()
    place = rows[...] * col_blocks + cols[...]
    slot_at = lax.broadcasted_iota(jnp.int32, (lanes, lanes), 0)
    lane_at = lax.broadcasted_iota(jnp.int32, (lanes, lanes), 1)
    columns = [
        jnp.transpose(jnp.broadcast_to(place[s : s + 1], (lanes, lanes)))
        for s in range(slots // lanes)
    ]
    for t in range(table.shape[0]):
        found = jnp.full((1, lanes), slots, jnp.int32)
        for s, column in enumerate(columns):
            slot = slot_at + s * lanes
            hit = (column == lane_at + t * lanes) & (slot < counts[0])
            found += jnp.sum(jnp.where(hit, slot - slots, 0), axis=0, keepdims=True)
        table_rows[t : t + 1] = found
    table_copy = pltpu.make_async_copy(table_rows, table, load_sems.at[2])
    table_copy.start()
    table_copy.wait()
    grads_copy.wait()
    for i in range(V_PIECES):
        values_copy(i).wait()

    def block(row_block, col_block):
        at = row_block * col_blocks + col_block
        return values[table[at // lanes, at % lanes]]

    def partial(owner):
        total = jnp.zeros((examples, width), jnp.float32)
        for r in range(0, row_blocks, 2):
            tile = jnp.concatenate(
                [
                    jnp.concatenate([block(r + i, owner * wide + j) for j in range(wide)], axis=1)
                    for i in range(2)
                ],
                axis=0,
            )
            total += jnp.dot(
                grads[:, r * side : (r + 2) * side], tile, preferred_element_type=jnp.float32
            )
        return total

    def pair_copy(k):
        return remote(pair_out.at[k], pair_in.at[k], pair_send.at[k], pair_recv.at[k], sibling)

    def near_copy(k):
        return remote(near_out.at[k], near_in.at[k], near_send.at[k], near_recv.at[k], across)

    def far_copy(k):
        to = device((z + 1 + k) % depth, y, core)
        return remote(far_out.at[k], far_in.at[k], far_send.at[k], far_recv.at[k], to)

    def for_sibling(k, _):
        pair_out[k] = partial(device((z + 1 + k) % depth, (y + 1 + k // depth) % 2, 1 - core))
        pair_copy(k).start()
        return 0

    def pass_one(k):
        which = device((z + depth - k) % depth, y, core)
        query_copy(which, across, pass_near.at[k]).wait_recv()
        query_copy(which, across, pass_near.at[k]).start()
        query_copy(which, sibling, pass_far.at[k]).start()

    lax.fori_loop(0, 2 * depth, for_sibling, 0)
    pass_one(1)

    def for_near(k, _):
        total = partial(device((z + 1 + k) % depth, 1 - y, core))
        pair_copy(k).wait_recv()
        near_out[k] = (total + pair_in[k]).astype(jnp.bfloat16)
        near_copy(k).start()
        return 0

    lax.fori_loop(0, depth, for_near, 0)
    for k in range(2, depth - 1):
        pass_one(k)

    def for_far(k):
        total = partial(device((z + 1 + k) % depth, y, core))
        pair_copy(depth + k).wait_recv()
        near_copy(k).wait_recv()
        return total + pair_in[depth + k] + near_in[k].astype(jnp.float32)

    def send_far(k, _):
        far_out[k] = for_far(k).astype(jnp.bfloat16)
        far_copy(k).start()
        return 0

    lax.fori_loop(0, depth - 1, send_far, 0)
    pass_one(depth - 1)
    features = for_far(depth - 1)

    def pass_across(k, _):
        which = device((z + depth - k) % depth, 1 - y, core)
        query_copy(which, sibling, pass_pair.at[k]).wait_recv()
        query_copy(which, sibling, pass_pair.at[k]).start()
        return 0

    lax.fori_loop(0, depth, pass_across, 0)

    def wait_passed(k, _):
        query_copy(2 * k + 1 - core, sibling, query_send.at[0]).wait_recv()
        return 0

    lax.fori_loop(0, 2 * depth, wait_passed, 0)
    gram_copy.wait()

    stacked = all_queries[...].reshape(n * 2 * query_rows, half)
    contract = (((1,), (1,)), ((), ()))
    first = lax.dot_general(gram[:, :half], stacked, contract, preferred_element_type=jnp.float32)
    second = lax.dot_general(gram[:, half:], stacked, contract, preferred_element_type=jnp.float32)
    across_all = n * 2 * query_rows
    whitened = (first + pltpu.roll(second, across_all - query_rows, 1)).astype(jnp.bfloat16)
    row = lax.broadcasted_iota(jnp.int32, (across_all, n * query_rows), 0)
    col = lax.broadcasted_iota(jnp.int32, (across_all, n * query_rows), 1)
    pick = (row == (col // query_rows) * (2 * query_rows) + col % query_rows).astype(jnp.bfloat16)
    whitened = jnp.dot(whitened, pick, preferred_element_type=jnp.float32).astype(jnp.bfloat16)

    for k in range(depth - 1):
        far_copy(k).wait_recv()
        features += far_in[k].astype(jnp.float32)
    high = features.astype(jnp.bfloat16)
    rest = features - high.astype(jnp.float32)
    middle = rest.astype(jnp.bfloat16)
    low = (rest - middle.astype(jnp.float32)).astype(jnp.bfloat16)
    scores = jnp.dot(high, whitened, preferred_element_type=jnp.float32)
    scores += jnp.dot(middle, whitened, preferred_element_type=jnp.float32)
    scores += jnp.dot(low, whitened, preferred_element_type=jnp.float32)
    for d in range(n):
        score_out[d, :out_rows, :] = scores[d * out_rows : (d + 1) * out_rows]

    def score_copy(k):
        to = (me + k) % n
        return remote(score_out.at[to], score_in.at[k], score_send.at[k], score_recv.at[k], to)

    def send_scores(k, _):
        score_copy(k).start()
        return 0

    lax.fori_loop(1, n, send_scores, 0)
    result = score_out[me]
    for k in range(1, n):
        score_copy(k).wait_recv()
        result += score_in[k]
    out[...] = result[:out_rows]

    def drain_pair(k, _):
        pair_copy(k).wait_send()
        return 0

    lax.fori_loop(0, 2 * depth, drain_pair, 0)

    def drain_depth(k, _):
        near_copy(k).wait_send()
        query_copy(me, sibling, query_send.at[k]).wait_send()
        query_copy(me, sibling, pass_pair.at[k]).wait_send()
        return 0

    lax.fori_loop(0, depth, drain_depth, 0)
    query_copy(me, sibling, query_send.at[depth]).wait_send()

    def drain_far(k, _):
        far_copy(k).wait_send()
        query_copy(me, sibling, pass_near.at[k + 1]).wait_send()
        query_copy(me, sibling, pass_far.at[k + 1]).wait_send()
        return 0

    lax.fori_loop(0, depth - 1, drain_far, 0)

    def drain_scores(k, _):
        score_copy(k).wait_send()
        return 0

    lax.fori_loop(1, n, drain_scores, 0)


def fused_shards(grads, block_values, block_rows, block_cols, block_counts, inv_gram, queries):
    n = lax.axis_size("blk")
    depth = n // 4
    examples, params = grads.shape
    slots, side = block_values.shape[0], block_values.shape[1]
    width, feature_dim = inv_gram.shape
    query_rows = queries.shape[0]
    out_rows = examples // n
    padded_rows = -(-out_rows // 8) * 8
    places = (params // side) * (feature_dim // side)
    lanes = 128
    vmem = pl.BlockSpec(memory_space=pltpu.VMEM)
    smem = pl.BlockSpec(memory_space=pltpu.SMEM)
    hbm = pl.BlockSpec(memory_space=pltpu.HBM)
    dma = pltpu.SemaphoreType.DMA
    return pl.pallas_call(
        functools.partial(fused_kernel, n),
        out_shape=jax.ShapeDtypeStruct((out_rows, n * query_rows), jnp.float32),
        in_specs=[hbm, hbm, smem, hbm, hbm, hbm, vmem],
        out_specs=vmem,
        scratch_shapes=[
            pltpu.VMEM((slots // lanes, lanes), jnp.int32),
            pltpu.VMEM((slots // lanes, lanes), jnp.int32),
            pltpu.VMEM((places // lanes, lanes), jnp.int32),
            pltpu.SMEM((places // lanes, lanes), jnp.int32),
            pltpu.VMEM((examples, params), jnp.bfloat16),
            pltpu.VMEM((slots + 1, side, side), jnp.bfloat16),
            pltpu.VMEM((width, feature_dim), jnp.bfloat16),
            pltpu.VMEM((n, 2 * query_rows, feature_dim // 2), jnp.bfloat16),
            pltpu.VMEM((2 * depth, examples, width), jnp.float32),
            pltpu.VMEM((2 * depth, examples, width), jnp.float32),
            pltpu.VMEM((depth, examples, width), jnp.bfloat16),
            pltpu.VMEM((depth, examples, width), jnp.bfloat16),
            pltpu.VMEM((depth, examples, width), jnp.bfloat16),
            pltpu.VMEM((depth, examples, width), jnp.bfloat16),
            pltpu.VMEM((n, padded_rows, n * query_rows), jnp.float32),
            pltpu.VMEM((n, padded_rows, n * query_rows), jnp.float32),
            dma((2,)),
            dma((V_PIECES,)),
            dma((3,)),
            dma((depth + 1,)),
            dma((n,)),
            dma((depth,)),
            dma((depth,)),
            dma((depth,)),
            dma((2 * depth,)),
            dma((2 * depth,)),
            dma((depth,)),
            dma((depth,)),
            dma((depth,)),
            dma((depth,)),
            dma((n,)),
            dma((n,)),
        ],
        compiler_params=pltpu.CompilerParams(
            collective_id=0, has_side_effects=True, vmem_limit_bytes=63 * 1024 * 1024
        ),
    )(
        block_rows.reshape(slots // lanes, lanes),
        block_cols.reshape(slots // lanes, lanes),
        block_counts,
        grads,
        block_values,
        inv_gram,
        queries,
    )


def fits(mesh, args):
    grads, block_values, _, _, _, inv_gram, queries = args
    n, groups = mesh.shape["blk"], mesh.shape["groups"]
    side = block_values.shape[1]
    width = inv_gram.shape[0] // n
    return (
        n % 4 == 0
        and n > 8
        and side == 128
        and width % side == 0
        and block_values.shape[0] // n % 128 == 0
        and grads.shape[1] // n % (2 * side) == 0
        and grads.shape[0] // groups % 16 == 0
        and queries.shape[0] // (groups * n) == 8
    )


def solution(mesh):
    placed = (
        P("groups", "blk"),
        P("blk", None, None),
        P("blk"),
        P("blk"),
        P("blk"),
        P("blk", None),
        P(("groups", "blk"), None),
    )

    def whole(*args):
        body = fused_shards if fits(mesh, args) else shards
        return jax.shard_map(
            body, mesh=mesh, in_specs=placed, out_specs=P(("groups", "blk"), None), check_vma=False
        )(*args)

    return whole
```

```python
import functools

import jax
import jax.numpy as jnp
from jax import lax
from jax.experimental import pallas as pl
from jax.experimental.pallas import tpu as pltpu
from jax.sharding import PartitionSpec as P

MESH = pl.DeviceIdType.MESH
V_PIECES = 8


def passed_along(value, axis, by):
    devices = lax.axis_size(axis)
    return lax.ppermute(value, axis, [(i, (i + by) % devices) for i in range(devices)])


def cycle_tiles(moving, make_tile):
    cycle_size = lax.axis_size("blk")
    position = lax.axis_index("blk")
    first_tile = make_tile(moving)
    tile_stack = jnp.zeros((cycle_size,) + first_tile.shape, jnp.float32)
    tile_stack = lax.dynamic_update_index_in_dim(tile_stack, first_tile, position, 0)

    def advance_one(step_index, carry):
        stack_now, current = carry
        current = passed_along(current, "blk", 1)
        stack_now = lax.dynamic_update_index_in_dim(
            stack_now, make_tile(current), (position - step_index) % cycle_size, 0
        )
        return (stack_now, current)

    tile_stack = lax.fori_loop(1, cycle_size, advance_one, (tile_stack, moving))[0]
    return tile_stack


def shards(grads, block_values, block_rows, block_cols, block_counts, inv_gram, queries):
    examples, param_width = grads.shape
    slot_count = block_values.shape[0]
    block_side = block_values.shape[1]
    feature_dim = inv_gram.shape[1]
    col_blocks = feature_dim // block_side
    tiled = grads.reshape(examples, param_width // block_side, block_side)
    slot_group = 64
    group_count = slot_count // slot_group
    live_slots = (jnp.arange(slot_count, dtype=jnp.int32) < block_counts[0]).astype(jnp.bfloat16)

    def add_group(totals, inputs):
        group_rows, group_cols, group_values, group_live = inputs
        selected = jnp.take(tiled, group_rows, axis=1)
        weights = group_values * group_live[:, None, None]
        products = jnp.einsum("ejb,jbc->ejc", selected, weights, preferred_element_type=jnp.float32)
        return (totals.at[:, group_cols, :].add(products), None)

    group_inputs = (
        block_rows.reshape(group_count, slot_group),
        block_cols.reshape(group_count, slot_group),
        block_values.reshape(group_count, slot_group, block_side, block_side),
        live_slots.reshape(group_count, slot_group),
    )
    start_totals = jnp.zeros((examples, col_blocks, block_side), jnp.float32)
    totals, unused = lax.scan(add_group, start_totals, group_inputs)
    partial_features = totals.reshape(examples, feature_dim)
    contract = (((1,), (1,)), ((), ()))

    def tile_for_queries(query_block):
        return lax.dot_general(inv_gram, query_block, contract, preferred_element_type=jnp.float32)

    tile_stack = cycle_tiles(queries, tile_for_queries)
    gram_rows = inv_gram.shape[0]
    whitened_queries = (
        jnp.transpose(tile_stack, (1, 0, 2)).reshape(gram_rows, -1).astype(jnp.bfloat16)
    )
    features = lax.psum_scatter(partial_features, "blk", scatter_dimension=1, tiled=True)
    query_float = whitened_queries.astype(jnp.float32)
    return lax.psum_scatter(
        jnp.dot(features, query_float, precision=lax.Precision.HIGHEST),
        "blk",
        scatter_dimension=0,
        tiled=True,
    )


def remote(src, dst, send_sem, recv_sem, device):
    return pltpu.make_async_remote_copy(
        src_ref=src,
        dst_ref=dst,
        send_sem=send_sem,
        recv_sem=recv_sem,
        device_id={"blk": device},
        device_id_type=MESH,
    )


def fused_kernel(
    n, rows_hbm, cols_hbm, counts, grads_hbm, values_hbm, gram_hbm, queries, out,
    rows, cols, table_rows, table, grads, values, gram, all_queries, pair_out, pair_in,
    near_out, near_in, far_out, far_in, score_out, score_in,
    slot_sems, values_sem, load_sems, query_send, query_recv, pass_near, pass_far, pass_pair,
    pair_send, pair_recv, near_send, near_recv, far_send, far_recv, score_send, score_recv,
):
    depth = n // 4
    me = lax.axis_index("blk")
    z, y, core = me // 4, (me // 2) % 2, me % 2

    def device(at_z, at_y, at_core):
        return 4 * at_z + 2 * at_y + at_core

    sibling = device(z, y, 1 - core)
    across = device(z, 1 - y, core)
    examples, params = grads.shape
    slots, side = values_hbm.shape[0], values_hbm.shape[1]
    width, feature_dim = gram.shape
    wide = width // side
    col_blocks = feature_dim // side
    row_blocks = params // side
    half = feature_dim // 2
    query_rows = queries.shape[0]
    out_rows = out.shape[0]
    piece = slots // V_PIECES
    lanes = rows.shape[1]

    barrier = pltpu.get_barrier_semaphore()

    peers = [sibling, across] + [device((z + k) % depth, y, core) for k in range(1, depth)]
    for peer in peers:
        pl.semaphore_signal(barrier, inc=1, device_id={"blk": peer}, device_id_type=MESH)

    rows_copy = pltpu.make_async_copy(rows_hbm, rows, slot_sems.at[0])
    cols_copy = pltpu.make_async_copy(cols_hbm, cols, slot_sems.at[1])
    rows_copy.start()
    cols_copy.start()

    def values_copy(i):
        part = pl.ds(i * piece, piece)
        return pltpu.make_async_copy(values_hbm.at[part], values.at[part], values_sem.at[i])

    grads_copy = pltpu.make_async_copy(grads_hbm, grads, load_sems.at[0])
    gram_copy = pltpu.make_async_copy(gram_hbm, gram, load_sems.at[1])
    grads_copy.start()
    for i in range(V_PIECES):
        values_copy(i).start()
    gram_copy.start()

    own_queries = queries[...].astype(jnp.float32)
    all_queries[me] = jnp.concatenate(
        [own_queries[:, :half], own_queries[:, half:]], axis=0
    ).astype(jnp.bfloat16)
    values[slots] = jnp.zeros((side, side), jnp.bfloat16)
    rows_copy.wait()
    cols_copy.wait()
    place = rows[...] * col_blocks + cols[...]
    slot_at = lax.broadcasted_iota(jnp.int32, (lanes, lanes), 0)
    lane_at = lax.broadcasted_iota(jnp.int32, (lanes, lanes), 1)
    columns = [
        jnp.transpose(jnp.broadcast_to(place[s : s + 1], (lanes, lanes)))
        for s in range(slots // lanes)
    ]
    for t in range(table.shape[0]):
        found = jnp.full((1, lanes), slots, jnp.int32)
        for s, column in enumerate(columns):
            slot = slot_at + s * lanes
            hit = (column == lane_at + t * lanes) & (slot < counts[0])
            found += jnp.sum(jnp.where(hit, slot - slots, 0), axis=0, keepdims=True)
        table_rows[t : t + 1] = found
    table_copy = pltpu.make_async_copy(table_rows, table, load_sems.at[2])
    table_copy.start()

    pl.semaphore_wait(barrier, len(peers))

    def query_copy(which, to, send_sem):
        return remote(all_queries.at[which], all_queries.at[which], send_sem, query_recv.at[which], to)

    def send_queries(k, _):
        query_copy(me, device((z + k) % depth, y, core), query_send.at[k]).start()
        return 0

    lax.fori_loop(1, depth, send_queries, 0)
    query_copy(me, across, query_send.at[depth]).start()
    query_copy(me, sibling, query_send.at[0]).start()

    table_copy.wait()
    grads_copy.wait()
    for i in range(V_PIECES):
        values_copy(i).wait()

    def block(row_block, col_block):
        at = row_block * col_blocks + col_block
        return values[table[at // lanes, at % lanes]]

    def partial(owner):
        total = jnp.zeros((examples, width), jnp.float32)
        for r in range(0, row_blocks, 2):
            tile = jnp.concatenate(
                [
                    jnp.concatenate([block(r + i, owner * wide + j) for j in range(wide)], axis=1)
                    for i in range(2)
                ],
                axis=0,
            )
            total += jnp.dot(
                grads[:, r * side : (r + 2) * side], tile, preferred_element_type=jnp.float32
            )
        return total

    def pair_copy(k):
        return remote(pair_out.at[k], pair_in.at[k], pair_send.at[k], pair_recv.at[k], sibling)

    def near_copy(k):
        return remote(near_out.at[k], near_in.at[k], near_send.at[k], near_recv.at[k], across)

    def far_copy(k):
        to = device((z + 1 + k) % depth, y, core)
        return remote(far_out.at[k], far_in.at[k], far_send.at[k], far_recv.at[k], to)

    def for_sibling(k, _):
        pair_out[k] = partial(device((z + 1 + k) % depth, (y + 1 + k // depth) % 2, 1 - core))
        pair_copy(k).start()
        return 0

    def pass_one(k):
        which = device((z + depth - k) % depth, y, core)
        query_copy(which, across, pass_near.at[k]).wait_recv()
        query_copy(which, across, pass_near.at[k]).start()
        query_copy(which, sibling, pass_far.at[k]).start()

    lax.fori_loop(0, depth, for_sibling, 0)

    def for_near(k, _):
        total = partial(device((z + 1 + k) % depth, 1 - y, core))
        pair_copy(k).wait_recv()
        near_out[k] = (total + pair_in[k]).astype(jnp.bfloat16)
        near_copy(k).start()
        return 0

    lax.fori_loop(0, depth, for_near, 0)
    lax.fori_loop(depth, 2 * depth, for_sibling, 0)
    for k in range(1, depth):
        pass_one(k)

    def for_far(k):
        total = partial(device((z + 1 + k) % depth, y, core))
        pair_copy(depth + k).wait_recv()
        near_copy(k).wait_recv()
        return total + pair_in[depth + k] + near_in[k].astype(jnp.float32)

    def send_far(k, _):
        far_out[k] = for_far(k).astype(jnp.bfloat16)
        far_copy(k).start()
        return 0

    lax.fori_loop(0, depth - 1, send_far, 0)
    features = for_far(depth - 1)

    def pass_across(k, _):
        which = device((z + depth - k) % depth, 1 - y, core)
        query_copy(which, sibling, pass_pair.at[k]).wait_recv()
        query_copy(which, sibling, pass_pair.at[k]).start()
        return 0

    lax.fori_loop(0, depth, pass_across, 0)

    def wait_passed(k, _):
        query_copy(2 * k + 1 - core, sibling, query_send.at[0]).wait_recv()
        return 0

    lax.fori_loop(0, 2 * depth, wait_passed, 0)
    gram_copy.wait()

    stacked = all_queries[...].reshape(n * 2 * query_rows, half)
    contract = (((1,), (1,)), ((), ()))
    first = lax.dot_general(gram[:, :half], stacked, contract, preferred_element_type=jnp.float32)
    second = lax.dot_general(gram[:, half:], stacked, contract, preferred_element_type=jnp.float32)
    across_all = n * 2 * query_rows
    whitened = (first + pltpu.roll(second, across_all - query_rows, 1)).astype(jnp.bfloat16)
    row = lax.broadcasted_iota(jnp.int32, (across_all, n * query_rows), 0)
    col = lax.broadcasted_iota(jnp.int32, (across_all, n * query_rows), 1)
    pick = (row == (col // query_rows) * (2 * query_rows) + col % query_rows).astype(jnp.bfloat16)
    whitened = jnp.dot(whitened, pick, preferred_element_type=jnp.float32).astype(jnp.bfloat16)

    for k in range(depth - 1):
        far_copy(k).wait_recv()
        features += far_in[k].astype(jnp.float32)
    high = features.astype(jnp.bfloat16)
    rest = features - high.astype(jnp.float32)
    middle = rest.astype(jnp.bfloat16)
    low = (rest - middle.astype(jnp.float32)).astype(jnp.bfloat16)
    scores = jnp.dot(high, whitened, preferred_element_type=jnp.float32)
    scores += jnp.dot(middle, whitened, preferred_element_type=jnp.float32)
    scores += jnp.dot(low, whitened, preferred_element_type=jnp.float32)
    for d in range(n):
        score_out[d, :out_rows, :] = scores[d * out_rows : (d + 1) * out_rows]

    def score_copy(k):
        to = (me + k) % n
        return remote(score_out.at[to], score_in.at[k], score_send.at[k], score_recv.at[k], to)

    def send_scores(k, _):
        score_copy(k).start()
        return 0

    lax.fori_loop(1, n, send_scores, 0)
    result = score_out[me]
    for k in range(1, n):
        score_copy(k).wait_recv()
        result += score_in[k]
    out[...] = result[:out_rows]

    def drain_pair(k, _):
        pair_copy(k).wait_send()
        return 0

    lax.fori_loop(0, 2 * depth, drain_pair, 0)

    def drain_depth(k, _):
        near_copy(k).wait_send()
        query_copy(me, sibling, query_send.at[k]).wait_send()
        query_copy(me, sibling, pass_pair.at[k]).wait_send()
        return 0

    lax.fori_loop(0, depth, drain_depth, 0)
    query_copy(me, sibling, query_send.at[depth]).wait_send()

    def drain_far(k, _):
        far_copy(k).wait_send()
        query_copy(me, sibling, pass_near.at[k + 1]).wait_send()
        query_copy(me, sibling, pass_far.at[k + 1]).wait_send()
        return 0

    lax.fori_loop(0, depth - 1, drain_far, 0)

    def drain_scores(k, _):
        score_copy(k).wait_send()
        return 0

    lax.fori_loop(1, n, drain_scores, 0)


def fused_shards(grads, block_values, block_rows, block_cols, block_counts, inv_gram, queries):
    n = lax.axis_size("blk")
    depth = n // 4
    examples, params = grads.shape
    slots, side = block_values.shape[0], block_values.shape[1]
    width, feature_dim = inv_gram.shape
    query_rows = queries.shape[0]
    out_rows = examples // n
    padded_rows = -(-out_rows // 8) * 8
    places = (params // side) * (feature_dim // side)
    lanes = 128
    vmem = pl.BlockSpec(memory_space=pltpu.VMEM)
    smem = pl.BlockSpec(memory_space=pltpu.SMEM)
    hbm = pl.BlockSpec(memory_space=pltpu.HBM)
    dma = pltpu.SemaphoreType.DMA
    return pl.pallas_call(
        functools.partial(fused_kernel, n),
        out_shape=jax.ShapeDtypeStruct((out_rows, n * query_rows), jnp.float32),
        in_specs=[hbm, hbm, smem, hbm, hbm, hbm, vmem],
        out_specs=vmem,
        scratch_shapes=[
            pltpu.VMEM((slots // lanes, lanes), jnp.int32),
            pltpu.VMEM((slots // lanes, lanes), jnp.int32),
            pltpu.VMEM((places // lanes, lanes), jnp.int32),
            pltpu.SMEM((places // lanes, lanes), jnp.int32),
            pltpu.VMEM((examples, params), jnp.bfloat16),
            pltpu.VMEM((slots + 1, side, side), jnp.bfloat16),
            pltpu.VMEM((width, feature_dim), jnp.bfloat16),
            pltpu.VMEM((n, 2 * query_rows, feature_dim // 2), jnp.bfloat16),
            pltpu.VMEM((2 * depth, examples, width), jnp.float32),
            pltpu.VMEM((2 * depth, examples, width), jnp.float32),
            pltpu.VMEM((depth, examples, width), jnp.bfloat16),
            pltpu.VMEM((depth, examples, width), jnp.bfloat16),
            pltpu.VMEM((depth, examples, width), jnp.bfloat16),
            pltpu.VMEM((depth, examples, width), jnp.bfloat16),
            pltpu.VMEM((n, padded_rows, n * query_rows), jnp.float32),
            pltpu.VMEM((n, padded_rows, n * query_rows), jnp.float32),
            dma((2,)),
            dma((V_PIECES,)),
            dma((3,)),
            dma((depth + 1,)),
            dma((n,)),
            dma((depth,)),
            dma((depth,)),
            dma((depth,)),
            dma((2 * depth,)),
            dma((2 * depth,)),
            dma((depth,)),
            dma((depth,)),
            dma((depth,)),
            dma((depth,)),
            dma((n,)),
            dma((n,)),
        ],
        compiler_params=pltpu.CompilerParams(
            collective_id=0, has_side_effects=True, vmem_limit_bytes=63 * 1024 * 1024
        ),
    )(
        block_rows.reshape(slots // lanes, lanes),
        block_cols.reshape(slots // lanes, lanes),
        block_counts,
        grads,
        block_values,
        inv_gram,
        queries,
    )


def fits(mesh, args):
    grads, block_values, _, _, _, inv_gram, queries = args
    n, groups = mesh.shape["blk"], mesh.shape["groups"]
    side = block_values.shape[1]
    width = inv_gram.shape[0] // n
    return (
        n % 4 == 0
        and n > 8
        and side == 128
        and width % side == 0
        and block_values.shape[0] // n % 128 == 0
        and grads.shape[1] // n % (2 * side) == 0
        and grads.shape[0] // groups % 16 == 0
        and queries.shape[0] // (groups * n) == 8
    )


def solution(mesh):
    placed = (
        P("groups", "blk"),
        P("blk", None, None),
        P("blk"),
        P("blk"),
        P("blk"),
        P("blk", None),
        P(("groups", "blk"), None),
    )

    def whole(*args):
        body = fused_shards if fits(mesh, args) else shards
        return jax.shard_map(
            body, mesh=mesh, in_specs=placed, out_specs=P(("groups", "blk"), None), check_vma=False
        )(*args)

    return whole
```

```python
import functools

import jax
import jax.numpy as jnp
from jax import lax
from jax.experimental import pallas as pl
from jax.experimental.pallas import tpu as pltpu
from jax.sharding import PartitionSpec as P

MESH = pl.DeviceIdType.MESH
V_PIECES = 8


def passed_along(value, axis, by):
    devices = lax.axis_size(axis)
    return lax.ppermute(value, axis, [(i, (i + by) % devices) for i in range(devices)])


def cycle_tiles(moving, make_tile):
    cycle_size = lax.axis_size("blk")
    position = lax.axis_index("blk")
    first_tile = make_tile(moving)
    tile_stack = jnp.zeros((cycle_size,) + first_tile.shape, jnp.float32)
    tile_stack = lax.dynamic_update_index_in_dim(tile_stack, first_tile, position, 0)

    def advance_one(step_index, carry):
        stack_now, current = carry
        current = passed_along(current, "blk", 1)
        stack_now = lax.dynamic_update_index_in_dim(
            stack_now, make_tile(current), (position - step_index) % cycle_size, 0
        )
        return (stack_now, current)

    tile_stack = lax.fori_loop(1, cycle_size, advance_one, (tile_stack, moving))[0]
    return tile_stack


def shards(grads, block_values, block_rows, block_cols, block_counts, inv_gram, queries):
    examples, param_width = grads.shape
    slot_count = block_values.shape[0]
    block_side = block_values.shape[1]
    feature_dim = inv_gram.shape[1]
    col_blocks = feature_dim // block_side
    tiled = grads.reshape(examples, param_width // block_side, block_side)
    slot_group = 64
    group_count = slot_count // slot_group
    live_slots = (jnp.arange(slot_count, dtype=jnp.int32) < block_counts[0]).astype(jnp.bfloat16)

    def add_group(totals, inputs):
        group_rows, group_cols, group_values, group_live = inputs
        selected = jnp.take(tiled, group_rows, axis=1)
        weights = group_values * group_live[:, None, None]
        products = jnp.einsum("ejb,jbc->ejc", selected, weights, preferred_element_type=jnp.float32)
        return (totals.at[:, group_cols, :].add(products), None)

    group_inputs = (
        block_rows.reshape(group_count, slot_group),
        block_cols.reshape(group_count, slot_group),
        block_values.reshape(group_count, slot_group, block_side, block_side),
        live_slots.reshape(group_count, slot_group),
    )
    start_totals = jnp.zeros((examples, col_blocks, block_side), jnp.float32)
    totals, unused = lax.scan(add_group, start_totals, group_inputs)
    partial_features = totals.reshape(examples, feature_dim)
    contract = (((1,), (1,)), ((), ()))

    def tile_for_queries(query_block):
        return lax.dot_general(inv_gram, query_block, contract, preferred_element_type=jnp.float32)

    tile_stack = cycle_tiles(queries, tile_for_queries)
    gram_rows = inv_gram.shape[0]
    whitened_queries = (
        jnp.transpose(tile_stack, (1, 0, 2)).reshape(gram_rows, -1).astype(jnp.bfloat16)
    )
    features = lax.psum_scatter(partial_features, "blk", scatter_dimension=1, tiled=True)
    query_float = whitened_queries.astype(jnp.float32)
    return lax.psum_scatter(
        jnp.dot(features, query_float, precision=lax.Precision.HIGHEST),
        "blk",
        scatter_dimension=0,
        tiled=True,
    )


def remote(src, dst, send_sem, recv_sem, device):
    return pltpu.make_async_remote_copy(
        src_ref=src,
        dst_ref=dst,
        send_sem=send_sem,
        recv_sem=recv_sem,
        device_id={"blk": device},
        device_id_type=MESH,
    )


def fused_kernel(
    n, rows_hbm, cols_hbm, counts, grads_hbm, values_hbm, gram_hbm, queries, out,
    rows, cols, table_rows, table, grads, values, gram, all_queries, pair_out, pair_in,
    near_out, near_in, far_out, far_in, score_out, score_in,
    slot_sems, values_sem, load_sems, query_send, query_recv, pass_near, pass_far, pass_pair,
    pair_send, pair_recv, near_send, near_recv, far_send, far_recv, score_send, score_recv,
):
    depth = n // 4
    me = lax.axis_index("blk")
    z, y, core = me // 4, (me // 2) % 2, me % 2

    def device(at_z, at_y, at_core):
        return 4 * at_z + 2 * at_y + at_core

    sibling = device(z, y, 1 - core)
    across = device(z, 1 - y, core)
    examples, params = grads.shape
    slots, side = values_hbm.shape[0], values_hbm.shape[1]
    width, feature_dim = gram.shape
    wide = width // side
    col_blocks = feature_dim // side
    row_blocks = params // side
    half = feature_dim // 2
    query_rows = queries.shape[0]
    out_rows = out.shape[0]
    piece = slots // V_PIECES
    lanes = rows.shape[1]

    barrier = pltpu.get_barrier_semaphore()

    peers = [sibling, across] + [device((z + k) % depth, y, core) for k in range(1, depth)]
    for peer in peers:
        pl.semaphore_signal(barrier, inc=1, device_id={"blk": peer}, device_id_type=MESH)

    rows_copy = pltpu.make_async_copy(rows_hbm, rows, slot_sems.at[0])
    cols_copy = pltpu.make_async_copy(cols_hbm, cols, slot_sems.at[1])
    rows_copy.start()
    cols_copy.start()

    def values_copy(i):
        part = pl.ds(i * piece, piece)
        return pltpu.make_async_copy(values_hbm.at[part], values.at[part], values_sem.at[i])

    grads_copy = pltpu.make_async_copy(grads_hbm, grads, load_sems.at[0])
    gram_copy = pltpu.make_async_copy(gram_hbm, gram, load_sems.at[1])
    grads_copy.start()
    for i in range(V_PIECES):
        values_copy(i).start()
    gram_copy.start()

    own_queries = queries[...].astype(jnp.float32)
    all_queries[me] = jnp.concatenate(
        [own_queries[:, :half], own_queries[:, half:]], axis=0
    ).astype(jnp.bfloat16)
    values[slots] = jnp.zeros((side, side), jnp.bfloat16)
    rows_copy.wait()
    cols_copy.wait()
    place = rows[...] * col_blocks + cols[...]
    slot_at = lax.broadcasted_iota(jnp.int32, (lanes, lanes), 0)
    lane_at = lax.broadcasted_iota(jnp.int32, (lanes, lanes), 1)
    columns = [
        jnp.transpose(jnp.broadcast_to(place[s : s + 1], (lanes, lanes)))
        for s in range(slots // lanes)
    ]
    for t in range(table.shape[0]):
        found = jnp.full((1, lanes), slots, jnp.int32)
        for s, column in enumerate(columns):
            slot = slot_at + s * lanes
            hit = (column == lane_at + t * lanes) & (slot < counts[0])
            found += jnp.sum(jnp.where(hit, slot - slots, 0), axis=0, keepdims=True)
        table_rows[t : t + 1] = found
    table_copy = pltpu.make_async_copy(table_rows, table, load_sems.at[2])
    table_copy.start()

    pl.semaphore_wait(barrier, len(peers))

    def query_copy(which, to, send_sem):
        return remote(all_queries.at[which], all_queries.at[which], send_sem, query_recv.at[which], to)

    def send_queries(k, _):
        query_copy(me, device((z + k) % depth, y, core), query_send.at[k]).start()
        return 0

    lax.fori_loop(1, depth, send_queries, 0)
    query_copy(me, across, query_send.at[depth]).start()
    query_copy(me, sibling, query_send.at[0]).start()

    table_copy.wait()
    grads_copy.wait()
    for i in range(V_PIECES):
        values_copy(i).wait()

    def block(row_block, col_block):
        at = row_block * col_blocks + col_block
        return values[table[at // lanes, at % lanes]]

    def partial(owner):
        total = jnp.zeros((examples, width), jnp.float32)
        for r in range(0, row_blocks, 2):
            tile = jnp.concatenate(
                [
                    jnp.concatenate([block(r + i, owner * wide + j) for j in range(wide)], axis=1)
                    for i in range(2)
                ],
                axis=0,
            )
            total += jnp.dot(
                grads[:, r * side : (r + 2) * side], tile, preferred_element_type=jnp.float32
            )
        return total

    def pair_copy(k):
        return remote(pair_out.at[k], pair_in.at[k], pair_send.at[k], pair_recv.at[k], sibling)

    def near_copy(k):
        return remote(near_out.at[k], near_in.at[k], near_send.at[k], near_recv.at[k], across)

    def far_copy(k):
        to = device((z + 1 + k) % depth, y, core)
        return remote(far_out.at[k], far_in.at[k], far_send.at[k], far_recv.at[k], to)

    def for_sibling(k, _):
        pair_out[k] = partial(device((z + 1 + k) % depth, (y + 1 + k // depth) % 2, 1 - core))
        pair_copy(k).start()
        return 0

    def pass_one(k):
        which = device((z + depth - k) % depth, y, core)
        query_copy(which, across, pass_near.at[k]).wait_recv()
        query_copy(which, across, pass_near.at[k]).start()
        query_copy(which, sibling, pass_far.at[k]).start()

    lax.fori_loop(0, depth, for_sibling, 0)

    def for_near(k, _):
        total = partial(device((z + 1 + k) % depth, 1 - y, core))
        pair_copy(k).wait_recv()
        near_out[k] = (total + pair_in[k]).astype(jnp.bfloat16)
        near_copy(k).start()
        return 0

    lax.fori_loop(0, depth, for_near, 0)
    lax.fori_loop(depth, 2 * depth, for_sibling, 0)
    for k in range(1, depth):
        pass_one(k)

    def for_far(k):
        total = partial(device((z + 1 + k) % depth, y, core))
        pair_copy(depth + k).wait_recv()
        near_copy(k).wait_recv()
        return total + pair_in[depth + k] + near_in[k].astype(jnp.float32)

    def send_far(k, _):
        far_out[k] = for_far(k).astype(jnp.bfloat16)
        far_copy(k).start()
        return 0

    lax.fori_loop(0, depth - 1, send_far, 0)
    features = for_far(depth - 1)

    def pass_across(k, _):
        which = device((z + depth - k) % depth, 1 - y, core)
        query_copy(which, sibling, pass_pair.at[k]).wait_recv()
        query_copy(which, sibling, pass_pair.at[k]).start()
        return 0

    lax.fori_loop(0, depth, pass_across, 0)

    across_all = n * 2 * query_rows
    row = lax.broadcasted_iota(jnp.int32, (across_all, n * query_rows), 0)
    col = lax.broadcasted_iota(jnp.int32, (across_all, n * query_rows), 1)
    pick = (row == (col // query_rows) * (2 * query_rows) + col % query_rows).astype(jnp.bfloat16)
    for k in range(depth - 1):
        far_copy(k).wait_recv()
        features += far_in[k].astype(jnp.float32)
    high = features.astype(jnp.bfloat16)
    rest = features - high.astype(jnp.float32)
    middle = rest.astype(jnp.bfloat16)
    low = (rest - middle.astype(jnp.float32)).astype(jnp.bfloat16)

    def wait_passed(k, _):
        query_copy(2 * k + 1 - core, sibling, query_send.at[0]).wait_recv()
        return 0

    lax.fori_loop(0, 2 * depth, wait_passed, 0)
    gram_copy.wait()

    stacked = all_queries[...].reshape(n * 2 * query_rows, half)
    contract = (((1,), (1,)), ((), ()))
    first = lax.dot_general(gram[:, :half], stacked, contract, preferred_element_type=jnp.float32)
    second = lax.dot_general(gram[:, half:], stacked, contract, preferred_element_type=jnp.float32)
    whitened = (first + pltpu.roll(second, across_all - query_rows, 1)).astype(jnp.bfloat16)
    whitened = jnp.dot(whitened, pick, preferred_element_type=jnp.float32).astype(jnp.bfloat16)

    scores = jnp.dot(high, whitened, preferred_element_type=jnp.float32)
    scores += jnp.dot(middle, whitened, preferred_element_type=jnp.float32)
    scores += jnp.dot(low, whitened, preferred_element_type=jnp.float32)
    for d in range(n):
        score_out[d, :out_rows, :] = scores[d * out_rows : (d + 1) * out_rows]

    def score_copy(k):
        to = (me + k) % n
        return remote(score_out.at[to], score_in.at[k], score_send.at[k], score_recv.at[k], to)

    def send_scores(k, _):
        score_copy(k).start()
        return 0

    lax.fori_loop(1, n, send_scores, 0)

    def drain_pair(k, _):
        pair_copy(k).wait_send()
        return 0

    lax.fori_loop(0, 2 * depth, drain_pair, 0)

    def drain_depth(k, _):
        near_copy(k).wait_send()
        query_copy(me, sibling, query_send.at[k]).wait_send()
        query_copy(me, sibling, pass_pair.at[k]).wait_send()
        return 0

    lax.fori_loop(0, depth, drain_depth, 0)
    query_copy(me, sibling, query_send.at[depth]).wait_send()

    def drain_far(k, _):
        far_copy(k).wait_send()
        query_copy(me, sibling, pass_near.at[k + 1]).wait_send()
        query_copy(me, sibling, pass_far.at[k + 1]).wait_send()
        return 0

    lax.fori_loop(0, depth - 1, drain_far, 0)

    result = score_out[me]
    for k in range(1, n):
        score_copy(k).wait_recv()
        result += score_in[k]
    out[...] = result[:out_rows]

    def drain_scores(k, _):
        score_copy(k).wait_send()
        return 0

    lax.fori_loop(1, n, drain_scores, 0)


def fused_shards(grads, block_values, block_rows, block_cols, block_counts, inv_gram, queries):
    n = lax.axis_size("blk")
    depth = n // 4
    examples, params = grads.shape
    slots, side = block_values.shape[0], block_values.shape[1]
    width, feature_dim = inv_gram.shape
    query_rows = queries.shape[0]
    out_rows = examples // n
    padded_rows = -(-out_rows // 8) * 8
    places = (params // side) * (feature_dim // side)
    lanes = 128
    vmem = pl.BlockSpec(memory_space=pltpu.VMEM)
    smem = pl.BlockSpec(memory_space=pltpu.SMEM)
    hbm = pl.BlockSpec(memory_space=pltpu.HBM)
    dma = pltpu.SemaphoreType.DMA
    return pl.pallas_call(
        functools.partial(fused_kernel, n),
        out_shape=jax.ShapeDtypeStruct((out_rows, n * query_rows), jnp.float32),
        in_specs=[hbm, hbm, smem, hbm, hbm, hbm, vmem],
        out_specs=vmem,
        scratch_shapes=[
            pltpu.VMEM((slots // lanes, lanes), jnp.int32),
            pltpu.VMEM((slots // lanes, lanes), jnp.int32),
            pltpu.VMEM((places // lanes, lanes), jnp.int32),
            pltpu.SMEM((places // lanes, lanes), jnp.int32),
            pltpu.VMEM((examples, params), jnp.bfloat16),
            pltpu.VMEM((slots + 1, side, side), jnp.bfloat16),
            pltpu.VMEM((width, feature_dim), jnp.bfloat16),
            pltpu.VMEM((n, 2 * query_rows, feature_dim // 2), jnp.bfloat16),
            pltpu.VMEM((2 * depth, examples, width), jnp.float32),
            pltpu.VMEM((2 * depth, examples, width), jnp.float32),
            pltpu.VMEM((depth, examples, width), jnp.bfloat16),
            pltpu.VMEM((depth, examples, width), jnp.bfloat16),
            pltpu.VMEM((depth, examples, width), jnp.bfloat16),
            pltpu.VMEM((depth, examples, width), jnp.bfloat16),
            pltpu.VMEM((n, padded_rows, n * query_rows), jnp.float32),
            pltpu.VMEM((n, padded_rows, n * query_rows), jnp.float32),
            dma((2,)),
            dma((V_PIECES,)),
            dma((3,)),
            dma((depth + 1,)),
            dma((n,)),
            dma((depth,)),
            dma((depth,)),
            dma((depth,)),
            dma((2 * depth,)),
            dma((2 * depth,)),
            dma((depth,)),
            dma((depth,)),
            dma((depth,)),
            dma((depth,)),
            dma((n,)),
            dma((n,)),
        ],
        compiler_params=pltpu.CompilerParams(
            collective_id=0, has_side_effects=True, vmem_limit_bytes=63 * 1024 * 1024
        ),
    )(
        block_rows.reshape(slots // lanes, lanes),
        block_cols.reshape(slots // lanes, lanes),
        block_counts,
        grads,
        block_values,
        inv_gram,
        queries,
    )


def fits(mesh, args):
    grads, block_values, _, _, _, inv_gram, queries = args
    n, groups = mesh.shape["blk"], mesh.shape["groups"]
    side = block_values.shape[1]
    width = inv_gram.shape[0] // n
    return (
        n % 4 == 0
        and n > 8
        and side == 128
        and width % side == 0
        and block_values.shape[0] // n % 128 == 0
        and grads.shape[1] // n % (2 * side) == 0
        and grads.shape[0] // groups % 16 == 0
        and queries.shape[0] // (groups * n) == 8
    )


def solution(mesh):
    placed = (
        P("groups", "blk"),
        P("blk", None, None),
        P("blk"),
        P("blk"),
        P("blk"),
        P("blk", None),
        P(("groups", "blk"), None),
    )

    def whole(*args):
        body = fused_shards if fits(mesh, args) else shards
        return jax.shard_map(
            body, mesh=mesh, in_specs=placed, out_specs=P(("groups", "blk"), None), check_vma=False
        )(*args)

    return whole
```

```python
import functools

import jax
import jax.numpy as jnp
from jax import lax
from jax.experimental import pallas as pl
from jax.experimental.pallas import tpu as pltpu
from jax.sharding import PartitionSpec as P

MESH = pl.DeviceIdType.MESH
V_PIECES = 8


def passed_along(value, axis, by):
    devices = lax.axis_size(axis)
    return lax.ppermute(value, axis, [(i, (i + by) % devices) for i in range(devices)])


def cycle_tiles(moving, make_tile):
    cycle_size = lax.axis_size("blk")
    position = lax.axis_index("blk")
    first_tile = make_tile(moving)
    tile_stack = jnp.zeros((cycle_size,) + first_tile.shape, jnp.float32)
    tile_stack = lax.dynamic_update_index_in_dim(tile_stack, first_tile, position, 0)

    def advance_one(step_index, carry):
        stack_now, current = carry
        current = passed_along(current, "blk", 1)
        stack_now = lax.dynamic_update_index_in_dim(
            stack_now, make_tile(current), (position - step_index) % cycle_size, 0
        )
        return (stack_now, current)

    tile_stack = lax.fori_loop(1, cycle_size, advance_one, (tile_stack, moving))[0]
    return tile_stack


def shards(grads, block_values, block_rows, block_cols, block_counts, inv_gram, queries):
    examples, param_width = grads.shape
    slot_count = block_values.shape[0]
    block_side = block_values.shape[1]
    feature_dim = inv_gram.shape[1]
    col_blocks = feature_dim // block_side
    tiled = grads.reshape(examples, param_width // block_side, block_side)
    slot_group = 64
    group_count = slot_count // slot_group
    live_slots = (jnp.arange(slot_count, dtype=jnp.int32) < block_counts[0]).astype(jnp.bfloat16)

    def add_group(totals, inputs):
        group_rows, group_cols, group_values, group_live = inputs
        selected = jnp.take(tiled, group_rows, axis=1)
        weights = group_values * group_live[:, None, None]
        products = jnp.einsum("ejb,jbc->ejc", selected, weights, preferred_element_type=jnp.float32)
        return (totals.at[:, group_cols, :].add(products), None)

    group_inputs = (
        block_rows.reshape(group_count, slot_group),
        block_cols.reshape(group_count, slot_group),
        block_values.reshape(group_count, slot_group, block_side, block_side),
        live_slots.reshape(group_count, slot_group),
    )
    start_totals = jnp.zeros((examples, col_blocks, block_side), jnp.float32)
    totals, unused = lax.scan(add_group, start_totals, group_inputs)
    partial_features = totals.reshape(examples, feature_dim)
    contract = (((1,), (1,)), ((), ()))

    def tile_for_queries(query_block):
        return lax.dot_general(inv_gram, query_block, contract, preferred_element_type=jnp.float32)

    tile_stack = cycle_tiles(queries, tile_for_queries)
    gram_rows = inv_gram.shape[0]
    whitened_queries = (
        jnp.transpose(tile_stack, (1, 0, 2)).reshape(gram_rows, -1).astype(jnp.bfloat16)
    )
    features = lax.psum_scatter(partial_features, "blk", scatter_dimension=1, tiled=True)
    query_float = whitened_queries.astype(jnp.float32)
    return lax.psum_scatter(
        jnp.dot(features, query_float, precision=lax.Precision.HIGHEST),
        "blk",
        scatter_dimension=0,
        tiled=True,
    )


def remote(src, dst, send_sem, recv_sem, device):
    return pltpu.make_async_remote_copy(
        src_ref=src,
        dst_ref=dst,
        send_sem=send_sem,
        recv_sem=recv_sem,
        device_id={"blk": device},
        device_id_type=MESH,
    )


def fused_kernel(
    n, rows_hbm, cols_hbm, counts, grads_hbm, values_hbm, gram_hbm, queries, out,
    rows, cols, table_rows, table, grads, values, gram, all_queries, pair_out, pair_in,
    near_out, near_in, far_out, far_in, score_out, score_in,
    slot_sems, values_sem, load_sems, query_send, query_recv, pass_near, pass_far, pass_pair,
    pair_send, pair_recv, near_send, near_recv, far_send, far_recv, score_send, score_recv,
):
    depth = n // 4
    chips = n // 2
    me = lax.axis_index("blk")
    z, y, core = me // 4, (me // 2) % 2, me % 2

    def device(at_z, at_y, at_core):
        return 4 * at_z + 2 * at_y + at_core

    sibling = device(z, y, 1 - core)
    across = device(z, 1 - y, core)
    examples, params = grads.shape
    slots, side = values_hbm.shape[0], values_hbm.shape[1]
    width, feature_dim = gram.shape
    wide = width // side
    col_blocks = feature_dim // side
    row_blocks = params // side
    half = feature_dim // 2
    query_rows = queries.shape[0]
    out_rows = out.shape[0]
    piece = slots // V_PIECES
    lanes = rows.shape[1]

    barrier = pltpu.get_barrier_semaphore()

    peers = [sibling, across] + [device((z + k) % depth, y, core) for k in range(1, depth)]
    for peer in peers:
        pl.semaphore_signal(barrier, inc=1, device_id={"blk": peer}, device_id_type=MESH)

    rows_copy = pltpu.make_async_copy(rows_hbm, rows, slot_sems.at[0])
    cols_copy = pltpu.make_async_copy(cols_hbm, cols, slot_sems.at[1])
    rows_copy.start()
    cols_copy.start()

    def values_copy(i):
        part = pl.ds(i * piece, piece)
        return pltpu.make_async_copy(values_hbm.at[part], values.at[part], values_sem.at[i])

    grads_copy = pltpu.make_async_copy(grads_hbm, grads, load_sems.at[0])
    gram_copy = pltpu.make_async_copy(gram_hbm, gram, load_sems.at[1])
    grads_copy.start()
    for i in range(V_PIECES):
        values_copy(i).start()
    gram_copy.start()

    own_queries = queries[...].astype(jnp.float32)
    all_queries[me] = jnp.concatenate(
        [own_queries[:, :half], own_queries[:, half:]], axis=0
    ).astype(jnp.bfloat16)
    values[slots] = jnp.zeros((side, side), jnp.bfloat16)
    rows_copy.wait()
    cols_copy.wait()
    place = rows[...] * col_blocks + cols[...]
    slot_at = lax.broadcasted_iota(jnp.int32, (lanes, lanes), 0)
    lane_at = lax.broadcasted_iota(jnp.int32, (lanes, lanes), 1)
    columns = [
        jnp.transpose(jnp.broadcast_to(place[s : s + 1], (lanes, lanes)))
        for s in range(slots // lanes)
    ]
    for t in range(table.shape[0]):
        found = jnp.full((1, lanes), slots, jnp.int32)
        for s, column in enumerate(columns):
            slot = slot_at + s * lanes
            hit = (column == lane_at + t * lanes) & (slot < counts[0])
            found += jnp.sum(jnp.where(hit, slot - slots, 0), axis=0, keepdims=True)
        table_rows[t : t + 1] = found
    table_copy = pltpu.make_async_copy(table_rows, table, load_sems.at[2])
    table_copy.start()

    pl.semaphore_wait(barrier, len(peers))

    def query_copy(which, to, send_sem):
        return remote(all_queries.at[which], all_queries.at[which], send_sem, query_recv.at[which], to)

    def send_queries(k, _):
        query_copy(me, device((z + k) % depth, y, core), query_send.at[k]).start()
        return 0

    lax.fori_loop(1, depth, send_queries, 0)
    query_copy(me, across, query_send.at[depth]).start()
    query_copy(me, sibling, query_send.at[0]).start()

    table_copy.wait()
    grads_copy.wait()
    for i in range(V_PIECES):
        values_copy(i).wait()

    def block(row_block, col_block):
        at = row_block * col_blocks + col_block
        return values[table[at // lanes, at % lanes]]

    def partial(owner):
        total = jnp.zeros((examples, width), jnp.float32)
        for r in range(0, row_blocks, 2):
            tile = jnp.concatenate(
                [
                    jnp.concatenate([block(r + i, owner * wide + j) for j in range(wide)], axis=1)
                    for i in range(2)
                ],
                axis=0,
            )
            total += jnp.dot(
                grads[:, r * side : (r + 2) * side], tile, preferred_element_type=jnp.float32
            )
        return total

    def pair_copy(k):
        return remote(pair_out.at[k], pair_in.at[k], pair_send.at[k], pair_recv.at[k], sibling)

    def near_copy(k):
        return remote(near_out.at[k], near_in.at[k], near_send.at[k], near_recv.at[k], across)

    def far_copy(k):
        to = device((z + 1 + k) % depth, y, core)
        return remote(far_out.at[k], far_in.at[k], far_send.at[k], far_recv.at[k], to)

    def for_sibling(k, _):
        pair_out[k] = partial(device((z + 1 + k) % depth, (y + 1 + k // depth) % 2, 1 - core))
        pair_copy(k).start()
        return 0

    def pass_one(k):
        which = device((z + depth - k) % depth, y, core)
        query_copy(which, across, pass_near.at[k]).wait_recv()
        query_copy(which, across, pass_near.at[k]).start()
        query_copy(which, sibling, pass_far.at[k]).start()

    lax.fori_loop(0, depth, for_sibling, 0)

    def for_near(k, _):
        total = partial(device((z + 1 + k) % depth, 1 - y, core))
        pair_copy(k).wait_recv()
        near_out[k] = (total + pair_in[k]).astype(jnp.bfloat16)
        near_copy(k).start()
        return 0

    lax.fori_loop(0, depth, for_near, 0)
    lax.fori_loop(depth, 2 * depth, for_sibling, 0)
    for k in range(1, depth):
        pass_one(k)

    def for_far(k):
        total = partial(device((z + 1 + k) % depth, y, core))
        pair_copy(depth + k).wait_recv()
        near_copy(k).wait_recv()
        return total + pair_in[depth + k] + near_in[k].astype(jnp.float32)

    def send_far(k, _):
        far_out[k] = for_far(k).astype(jnp.bfloat16)
        far_copy(k).start()
        return 0

    lax.fori_loop(0, depth - 1, send_far, 0)
    features = for_far(depth - 1)

    def pass_across(k, _):
        which = device((z + depth - k) % depth, 1 - y, core)
        query_copy(which, sibling, pass_pair.at[k]).wait_recv()
        query_copy(which, sibling, pass_pair.at[k]).start()
        return 0

    lax.fori_loop(0, depth, pass_across, 0)

    across_all = n * 2 * query_rows
    row = lax.broadcasted_iota(jnp.int32, (across_all, n * query_rows), 0)
    col = lax.broadcasted_iota(jnp.int32, (across_all, n * query_rows), 1)
    pick = (row == (col // query_rows) * (2 * query_rows) + col % query_rows).astype(jnp.bfloat16)
    for k in range(depth - 1):
        far_copy(k).wait_recv()
        features += far_in[k].astype(jnp.float32)
    high = features.astype(jnp.bfloat16)
    rest = features - high.astype(jnp.float32)
    middle = rest.astype(jnp.bfloat16)
    low = (rest - middle.astype(jnp.float32)).astype(jnp.bfloat16)

    def wait_passed(k, _):
        query_copy(2 * k + 1 - core, sibling, query_send.at[0]).wait_recv()
        return 0

    lax.fori_loop(0, 2 * depth, wait_passed, 0)
    gram_copy.wait()

    stacked = all_queries[...].reshape(n * 2 * query_rows, half)
    contract = (((1,), (1,)), ((), ()))
    first = lax.dot_general(gram[:, :half], stacked, contract, preferred_element_type=jnp.float32)
    second = lax.dot_general(gram[:, half:], stacked, contract, preferred_element_type=jnp.float32)
    whitened = (first + pltpu.roll(second, across_all - query_rows, 1)).astype(jnp.bfloat16)
    whitened = jnp.dot(whitened, pick, preferred_element_type=jnp.float32).astype(jnp.bfloat16)

    scores = jnp.dot(high, whitened, preferred_element_type=jnp.float32)
    scores += jnp.dot(middle, whitened, preferred_element_type=jnp.float32)
    scores += jnp.dot(low, whitened, preferred_element_type=jnp.float32)
    for d in range(n):
        score_out[(d % 2) * chips + d // 2, :out_rows, :] = scores[d * out_rows : (d + 1) * out_rows]

    theirs = pl.ds((1 - core) * chips, chips)
    ours = pl.ds(core * chips, chips)
    pair_scores = remote(
        score_out.at[theirs], score_in.at[pl.ds(0, chips)], score_send.at[0], score_recv.at[0], sibling
    )
    pair_scores.start()
    pair_scores.wait_recv()
    score_out[ours] = score_out[ours] + score_in[:chips]

    def score_copy(k):
        to = (me // 2 + k) % chips
        return remote(
            score_out.at[core * chips + to], score_in.at[chips + k],
            score_send.at[k], score_recv.at[k], 2 * to + core,
        )

    def send_scores(k, _):
        score_copy(k).start()
        return 0

    lax.fori_loop(1, chips, send_scores, 0)

    def drain_pair(k, _):
        pair_copy(k).wait_send()
        return 0

    lax.fori_loop(0, 2 * depth, drain_pair, 0)

    def drain_depth(k, _):
        near_copy(k).wait_send()
        query_copy(me, sibling, query_send.at[k]).wait_send()
        query_copy(me, sibling, pass_pair.at[k]).wait_send()
        return 0

    lax.fori_loop(0, depth, drain_depth, 0)
    query_copy(me, sibling, query_send.at[depth]).wait_send()

    def drain_far(k, _):
        far_copy(k).wait_send()
        query_copy(me, sibling, pass_near.at[k + 1]).wait_send()
        query_copy(me, sibling, pass_far.at[k + 1]).wait_send()
        return 0

    lax.fori_loop(0, depth - 1, drain_far, 0)

    result = score_out[core * chips + me // 2]
    for k in range(1, chips):
        score_copy(k).wait_recv()
        result += score_in[chips + k]
    out[...] = result[:out_rows]

    def drain_scores(k, _):
        score_copy(k).wait_send()
        return 0

    lax.fori_loop(1, chips, drain_scores, 0)
    pair_scores.wait_send()


def fused_shards(grads, block_values, block_rows, block_cols, block_counts, inv_gram, queries):
    n = lax.axis_size("blk")
    depth = n // 4
    examples, params = grads.shape
    slots, side = block_values.shape[0], block_values.shape[1]
    width, feature_dim = inv_gram.shape
    query_rows = queries.shape[0]
    out_rows = examples // n
    padded_rows = -(-out_rows // 8) * 8
    places = (params // side) * (feature_dim // side)
    lanes = 128
    vmem = pl.BlockSpec(memory_space=pltpu.VMEM)
    smem = pl.BlockSpec(memory_space=pltpu.SMEM)
    hbm = pl.BlockSpec(memory_space=pltpu.HBM)
    dma = pltpu.SemaphoreType.DMA
    return pl.pallas_call(
        functools.partial(fused_kernel, n),
        out_shape=jax.ShapeDtypeStruct((out_rows, n * query_rows), jnp.float32),
        in_specs=[hbm, hbm, smem, hbm, hbm, hbm, vmem],
        out_specs=vmem,
        scratch_shapes=[
            pltpu.VMEM((slots // lanes, lanes), jnp.int32),
            pltpu.VMEM((slots // lanes, lanes), jnp.int32),
            pltpu.VMEM((places // lanes, lanes), jnp.int32),
            pltpu.SMEM((places // lanes, lanes), jnp.int32),
            pltpu.VMEM((examples, params), jnp.bfloat16),
            pltpu.VMEM((slots + 1, side, side), jnp.bfloat16),
            pltpu.VMEM((width, feature_dim), jnp.bfloat16),
            pltpu.VMEM((n, 2 * query_rows, feature_dim // 2), jnp.bfloat16),
            pltpu.VMEM((2 * depth, examples, width), jnp.float32),
            pltpu.VMEM((2 * depth, examples, width), jnp.float32),
            pltpu.VMEM((depth, examples, width), jnp.bfloat16),
            pltpu.VMEM((depth, examples, width), jnp.bfloat16),
            pltpu.VMEM((depth, examples, width), jnp.bfloat16),
            pltpu.VMEM((depth, examples, width), jnp.bfloat16),
            pltpu.VMEM((n, padded_rows, n * query_rows), jnp.float32),
            pltpu.VMEM((n, padded_rows, n * query_rows), jnp.float32),
            dma((2,)),
            dma((V_PIECES,)),
            dma((3,)),
            dma((depth + 1,)),
            dma((n,)),
            dma((depth,)),
            dma((depth,)),
            dma((depth,)),
            dma((2 * depth,)),
            dma((2 * depth,)),
            dma((depth,)),
            dma((depth,)),
            dma((depth,)),
            dma((depth,)),
            dma((n,)),
            dma((n,)),
        ],
        compiler_params=pltpu.CompilerParams(
            collective_id=0, has_side_effects=True, vmem_limit_bytes=63 * 1024 * 1024
        ),
    )(
        block_rows.reshape(slots // lanes, lanes),
        block_cols.reshape(slots // lanes, lanes),
        block_counts,
        grads,
        block_values,
        inv_gram,
        queries,
    )


def fits(mesh, args):
    grads, block_values, _, _, _, inv_gram, queries = args
    n, groups = mesh.shape["blk"], mesh.shape["groups"]
    side = block_values.shape[1]
    width = inv_gram.shape[0] // n
    return (
        n % 4 == 0
        and n > 8
        and side == 128
        and width % side == 0
        and block_values.shape[0] // n % 128 == 0
        and grads.shape[1] // n % (2 * side) == 0
        and grads.shape[0] // groups % 16 == 0
        and queries.shape[0] // (groups * n) == 8
    )


def solution(mesh):
    placed = (
        P("groups", "blk"),
        P("blk", None, None),
        P("blk"),
        P("blk"),
        P("blk"),
        P("blk", None),
        P(("groups", "blk"), None),
    )

    def whole(*args):
        body = fused_shards if fits(mesh, args) else shards
        return jax.shard_map(
            body, mesh=mesh, in_specs=placed, out_specs=P(("groups", "blk"), None), check_vma=False
        )(*args)

    return whole
```
